1024 devices in a mesh: cap: 64 (over z_hi, y, x), vid: 16 (over z_lo, core).
Axes of the slice: x: 4, y: 8, z: 16 (z_hi: 2, z_lo: 8; z = z_hi * 8 + z_lo), core: 2. Of those that a mesh axis runs over, the one named last changes fastest.
Arguments:
- caption_tokens: bfloat16 [1024, 32, 128], P(('cap', 'vid')), may hold values from -12.1875 to 12.1875
- video_tokens: bfloat16 [1024, 128, 128], P(('cap', 'vid')), may hold values from -0.4875 to 0.4875
- row_norms: bfloat16 [1024], P(('cap', 'vid')), may hold values from 1 to 64, as said below
- col_norms: bfloat16 [1024], P(('cap', 'vid')), may hold values from 1 to 64, as said below
Outputs:
- caption_grads: bfloat16 [1024, 32, 128], P(('cap', 'vid'))
- video_grads: bfloat16 [1024, 128, 128], P(('cap', 'vid'))
The draws below stay inside these ranges and needn't reach their ends.
Inputs may be any that keep to these rules, and one draw needn't show every extreme that they name: `row_norms`: saved caption normalizers. `col_norms`: saved video normalizers.
All inputs are finite; a program needn't handle non-finite values.
Results may differ from the reference program's by a relative error of at most 0.015.
Values may be sent and summed in bfloat16 or wider, within the bound.
No kernel may reach another device: no remote copies, remote signals or barrier semaphores. Data moves between devices by JAX's collectives and lax.ppermute only.
A program may use at most 128 MiB of HBM per device.

```python
import math
import jax
import jax.numpy as jnp
from jax import lax

D = 128
LQ = 32
LV = 128
BATCH = 1024


def shared_part(key, salt):
    spread = (0.5 / D) ** 0.5
    return jax.random.uniform(jax.random.fold_in(key, salt), (D,), jnp.float32, -1.0, 1.0) * (spread * math.sqrt(3.0))


def video_normal(key):
    spread = (0.5 / D) ** 0.5
    rough = jnp.clip(jax.random.normal(jax.random.fold_in(key, 21), (BATCH, LV, D), jnp.float32), -6.0, 6.0) * spread
    return rough + shared_part(key, 25)[None, None, :]


def draw_video_tokens(key, part):
    base = video_normal(key)
    return base.astype(jnp.bfloat16)


def draw_caption_tokens(key, part):
    spread = (0.5 / D) ** 0.5
    common = shared_part(key, 26)
    own_key = jax.random.fold_in(key, 31)
    tokens = jnp.clip(jax.random.normal(own_key, (BATCH, LQ, D), jnp.float32), -6.0, 6.0) * spread
    tokens = tokens + common[None, None, :]
    return tokens.astype(jnp.bfloat16)


def logit_table(key, part):
    captions = draw_caption_tokens(key, part)
    videos = draw_video_tokens(key, part)
    block_size = min(16, BATCH)
    block_count = BATCH // block_size
    key_rows = videos.reshape(BATCH * LV, D)

    def advance(carry, index):
        start = (index * block_size).astype(jnp.int32)
        queries = lax.dynamic_slice_in_dim(captions, start, block_size, 0).reshape(block_size * LQ, D)
        scores = lax.dot_general(queries, key_rows, (((1,), (1,)), ((), ())), preferred_element_type=jnp.float32) / 0.05
        scores = scores.reshape(block_size, LQ, BATCH, LV)
        row_peak = jnp.max(scores, axis=3, keepdims=True)
        summed = jnp.sum(jnp.exp(scores - row_peak), axis=3)
        pooled = 0.05 * (row_peak[..., 0] + jnp.log(summed))
        return (carry, jnp.mean(pooled, axis=1) / 0.5)
    _, blocks = lax.scan(advance, jnp.zeros((), jnp.float32), jnp.arange(block_count, dtype=jnp.int32))
    return blocks.reshape(BATCH, BATCH)


def soft_total(logits, axis):
    peak = jnp.max(logits, axis=axis, keepdims=True)
    return jnp.squeeze(peak, axis) + jnp.log(jnp.sum(jnp.exp(logits - peak), axis=axis))


def draw_row_norms(key, part):
    logits = logit_table(key, part)
    own_key = jax.random.fold_in(key, 41)
    noise = jax.random.uniform(own_key, (BATCH,), jnp.float32, -0.1, 0.1)
    return (soft_total(logits, 1) + noise).astype(jnp.bfloat16)


def draw_col_norms(key, part):
    logits = logit_table(key, part)
    own_key = jax.random.fold_in(key, 42)
    noise = jax.random.uniform(own_key, (BATCH,), jnp.float32, -0.1, 0.1)
    return (soft_total(logits, 0) + noise).astype(jnp.bfloat16)


def setup_inputs(seed: int = 0) -> dict:
    arg_keys = jax.random.split(jax.random.key(seed), 5)
    return {
        "caption_tokens": draw_caption_tokens(jax.random.fold_in(arg_keys[4], 71), 0),
        "video_tokens": draw_video_tokens(jax.random.fold_in(arg_keys[4], 71), 0),
        "row_norms": draw_row_norms(jax.random.fold_in(arg_keys[4], 71), 0),
        "col_norms": draw_col_norms(jax.random.fold_in(arg_keys[4], 71), 0),
    }


pool_tau = 0.05
logit_temp = 0.5


def reference(caption_tokens, video_tokens, row_norms, col_norms):
    block_size = min(16, BATCH)
    block_count = BATCH // block_size
    key_rows = video_tokens.reshape(BATCH * LV, D)
    col_norm = col_norms.astype(jnp.float32)
    row_norm = row_norms.astype(jnp.float32)
    video_ids = jnp.arange(BATCH, dtype=jnp.int32)

    def advance(key_total, index):
        start = (index * block_size).astype(jnp.int32)
        captions = lax.dynamic_slice_in_dim(caption_tokens, start, block_size, 0)
        own_norm = lax.dynamic_slice_in_dim(row_norm, start, block_size, 0)
        caption_ids = start + jnp.arange(block_size, dtype=jnp.int32)
        queries = captions.reshape(block_size * LQ, D)
        scores = lax.dot_general(queries, key_rows, (((1,), (1,)), ((), ())), preferred_element_type=jnp.float32) / pool_tau
        scores = scores.reshape(block_size, LQ, BATCH, LV)
        row_peak = jnp.max(scores, axis=3, keepdims=True)
        lifted = jnp.exp(scores - row_peak)
        summed = jnp.sum(lifted, axis=3, keepdims=True)
        weights = lifted / summed
        pooled = pool_tau * (row_peak[..., 0] + jnp.log(summed[..., 0]))
        logits = jnp.mean(pooled, axis=1) / logit_temp
        positive = (caption_ids[:, None] == video_ids[None, :]).astype(jnp.float32)
        pair_grad = (jnp.exp(logits - own_norm[:, None]) + jnp.exp(logits - col_norm[None, :]) - 2.0 * positive) / (2.0 * logit_temp)
        token_coef = (pair_grad[:, None, :, None] * weights / LQ).astype(jnp.bfloat16)
        token_coef = token_coef.reshape(block_size * LQ, BATCH * LV)
        query_grad = jnp.dot(token_coef, key_rows, preferred_element_type=jnp.float32)
        key_total = key_total + lax.dot_general(token_coef, queries, (((0,), (0,)), ((), ())), preferred_element_type=jnp.float32)
        return key_total, query_grad.astype(jnp.bfloat16)

    key_total, query_grads = lax.scan(advance, jnp.zeros((BATCH * LV, D), jnp.float32), jnp.arange(block_count, dtype=jnp.int32))
    return query_grads.reshape(BATCH, LQ, D), key_total.reshape(BATCH, LV, D).astype(jnp.bfloat16)
```

```python
import functools
import math

import jax
import jax.numpy as jnp
from jax import lax
from jax.experimental import pallas as pl
from jax.experimental.pallas import tpu as pltpu
from jax.sharding import Mesh
from jax.sharding import PartitionSpec as P

pool_tau = 0.05
logit_temp = 0.5


def pair_kernel(
    caps_ref, vids_ref, dq_ref, dv_ref, own_dq_ref, own_dv_ref,
    lift_ref, coef_ref, peak_ref, sum_ref, turned_ref, total_ref, mine_ref, *, q_len, v_len, lanes,
):
    cap_rows, vid_rows = caps_ref.shape[0], vids_ref.shape[0]
    features = caps_ref.shape[2]
    block_caps = lanes // q_len
    blocks = cap_rows // block_caps
    to_exp2 = 1.0 / (pool_tau * math.log(2.0))

    own_cap = lax.axis_index("x") * lax.axis_size(Z) + lax.axis_index("z_hi") * lax.axis_size("z_lo") + lax.axis_index("z_lo")
    own_vid = lax.axis_index("core") * lax.axis_size("y") + lax.axis_index("y")
    cap_bits = block_caps.bit_length() - 1
    own_block, own_place = own_cap >> cap_bits, own_cap & (block_caps - 1)

    turned_ref[...] = vids_ref[:, :v_len, :].reshape(vid_rows * v_len, features).T
    total_ref[...] = jnp.zeros_like(total_ref)

    def queries_of(block):
        return caps_ref[pl.ds(block * block_caps, block_caps), :q_len, :].reshape(lanes, features)

    @pl.loop(0, blocks)
    def _(block):
        queries = queries_of(block)
        for v in range(vid_rows):
            scores = lax.dot_general(
                vids_ref[v, :v_len, :], queries, (((1,), (1,)), ((), ())), preferred_element_type=jnp.float32
            )
            peak = jnp.max(scores, axis=0, keepdims=True)
            lifted = jnp.exp2((scores - peak) * to_exp2)
            lift_ref[block, v] = lifted
            peak_ref[block, pl.ds(v, 1), :] = peak
            sum_ref[block, pl.ds(v, 1), :] = jnp.sum(lifted, axis=0, keepdims=True)

    q_bits = q_len.bit_length() - 1
    row = lax.broadcasted_iota(jnp.int32, (lanes, lanes), 0) >> q_bits
    col = lax.broadcasted_iota(jnp.int32, (lanes, lanes), 1) >> q_bits
    spread = jnp.where(row == col, 1.0 / (q_len * logit_temp), 0.0)
    col_norm = vids_ref[:, v_len, :1].astype(jnp.float32)
    lane_cap = lax.broadcasted_iota(jnp.int32, (vid_rows, lanes), 1) >> q_bits
    sub_vid = lax.broadcasted_iota(jnp.int32, (vid_rows, lanes), 0)

    mine_ref[...] = jnp.zeros_like(mine_ref)

    @pl.loop(0, blocks)
    def _(block):
        summed = sum_ref[block]
        pooled = peak_ref[block] + pool_tau * jnp.log(summed)
        logits = jnp.dot(pooled, spread, preferred_element_type=jnp.float32, precision=lax.Precision.HIGHEST)
        row_norm = jnp.zeros((1, lanes), jnp.float32)
        for c in range(block_caps):
            norm = caps_ref[block * block_caps + c, pl.ds(q_len, 1), :].astype(jnp.float32)
            norm = jnp.concatenate([norm] * (lanes // norm.shape[1]), axis=1)
            row_norm = jnp.where(lane_cap[:1] == c, norm, row_norm)
        paired = (lane_cap + block * block_caps == own_cap) & (sub_vid == own_vid)
        pair_grad = (jnp.exp(logits - row_norm) + jnp.exp(logits - col_norm) - 2.0 * paired.astype(jnp.float32)) / (2.0 * logit_temp)
        scale = pair_grad / (summed * q_len)
        sum_ref[block] = jnp.where(paired, 0.0, scale)
        mine_ref[...] += jnp.where(paired, scale, 0.0)

    @pl.loop(0, blocks)
    def _(block):
        queries = queries_of(block)
        for v in range(vid_rows):
            coef_ref[pl.ds(v * v_len, v_len), :] = (lift_ref[block, v] * sum_ref[block, pl.ds(v, 1), :]).astype(jnp.bfloat16)
        coef = coef_ref[...]
        turned = jnp.dot(turned_ref[...], coef, preferred_element_type=jnp.float32)
        dq_ref[pl.ds(block * block_caps, block_caps)] = turned.T.reshape(block_caps, q_len, features).astype(dq_ref.dtype)
        total_ref[...] += jnp.dot(coef, queries, preferred_element_type=jnp.float32)

    dv_ref[...] = total_ref[...].reshape(dv_ref.shape).astype(dv_ref.dtype)

    own_scale = jnp.sum(mine_ref[...], axis=0, keepdims=True)
    coef = (lift_ref[own_block, own_vid] * own_scale).astype(jnp.bfloat16)
    own_dv_ref[...] = jnp.dot(coef, queries_of(own_block), preferred_element_type=jnp.float32)
    total_ref[pl.ds(0, lanes), :] = lax.dot_general(
        coef, vids_ref[own_vid, :v_len, :], (((0,), (0,)), ((), ())), preferred_element_type=jnp.float32
    )
    own_dq_ref[...] = total_ref[pl.ds(own_place * q_len, q_len), :]


def pair_grads(caps, vids, q_len, v_len, lanes=256):
    cap_rows, vid_rows, features = caps.shape[0], vids.shape[0], caps.shape[2]
    blocks = cap_rows * q_len // lanes
    return pl.pallas_call(
        functools.partial(pair_kernel, q_len=q_len, v_len=v_len, lanes=lanes),
        out_shape=(
            jax.ShapeDtypeStruct((cap_rows, q_len, features), jnp.bfloat16),
            jax.ShapeDtypeStruct((vid_rows, v_len, features), jnp.bfloat16),
            jax.ShapeDtypeStruct((q_len, features), jnp.float32),
            jax.ShapeDtypeStruct((v_len, features), jnp.float32),
        ),
        in_specs=[
            pl.BlockSpec(memory_space=pltpu.VMEM),
            pl.BlockSpec(memory_space=pltpu.VMEM),
        ],
        out_specs=[pl.BlockSpec(memory_space=pltpu.VMEM)] * 4,
        scratch_shapes=[
            pltpu.VMEM((blocks, vid_rows, v_len, lanes), jnp.float32),
            pltpu.VMEM((vid_rows * v_len, lanes), jnp.bfloat16),
            pltpu.VMEM((blocks, vid_rows, lanes), jnp.float32),
            pltpu.VMEM((blocks, vid_rows, lanes), jnp.float32),
            pltpu.VMEM((features, vid_rows * v_len), jnp.bfloat16),
            pltpu.VMEM((vid_rows * v_len, features), jnp.float32),
            pltpu.VMEM((vid_rows, lanes), jnp.float32),
        ],
        compiler_params=pltpu.CompilerParams(vmem_limit_bytes=48 * 2**20),
        cost_estimate=pl.CostEstimate(
            flops=6 * cap_rows * q_len * vid_rows * v_len * features,
            bytes_accessed=4 * (cap_rows * q_len + vid_rows * v_len) * features,
            transcendentals=cap_rows * q_len * vid_rows * v_len,
        ),
    )(caps, vids)


PARTS = (2, 8, 4, 8, 2)
AXES = ("z_hi", "y", "x", "z_lo", "core")
Z = ("z_hi", "z_lo")


def with_norm(tokens, norm):
    return jnp.concatenate([tokens, jnp.broadcast_to(norm[:, None, None], (1, 8, tokens.shape[2]))], axis=1)


def spread_over(block, axis):
    size = lax.axis_size(axis)
    copies = jnp.broadcast_to(block[None], (size, *block.shape))
    return lax.all_to_all(copies, axis, 0, 0, tiled=True)


def sum_over(parts, axis):
    moved = lax.all_to_all(parts, axis, 0, 0, tiled=True)
    return jnp.sum(moved.astype(jnp.float32), axis=0)


def local(caption_tokens, video_tokens, row_norms, col_norms):
    q_len, v_len, features = caption_tokens.shape[1], video_tokens.shape[1], caption_tokens.shape[2]
    x_count, y_count, z_count = lax.axis_size("x"), lax.axis_size("y"), lax.axis_size(Z)
    caps = spread_over(with_norm(caption_tokens, row_norms)[0], Z)
    caps = spread_over(caps, "x").reshape(x_count * z_count, q_len + 8, features)
    vids = spread_over(with_norm(video_tokens, col_norms)[0], "y")
    vids = lax.all_gather(vids, "core", axis=0, tiled=True)
    dq, dv, own_dq, own_dv = pair_grads(caps, vids, q_len, v_len)
    dv = sum_over(dv.reshape(-1, y_count, v_len, features), "core").astype(jnp.bfloat16)
    dv = (sum_over(dv, "y") + own_dv).astype(jnp.bfloat16)
    dq = sum_over(dq.reshape(x_count, z_count, q_len, features), "x").astype(jnp.bfloat16)
    dq = (sum_over(dq, Z) + own_dq).astype(jnp.bfloat16)
    return dq[None], dv[None]


def solution(mesh):
    fine = Mesh(mesh.devices.reshape(PARTS), AXES)
    return jax.shard_map(
        local,
        mesh=fine,
        in_specs=(P(AXES, None, None), P(AXES, None, None), P(AXES), P(AXES)),
        out_specs=(P(AXES, None, None), P(AXES, None, None)),
        check_vma=False,
    )
```

```python
import functools
import math

import jax
import jax.numpy as jnp
from jax import lax
from jax.experimental import pallas as pl
from jax.experimental.pallas import tpu as pltpu
from jax.sharding import Mesh
from jax.sharding import PartitionSpec as P

pool_tau = 0.05
logit_temp = 0.5


def pair_kernel(
    caps_ref, vids_ref, dq_ref, own_dq_ref, dv_kept_ref, dv_sent_ref,
    lift_ref, coef_ref, peak_ref, sum_ref, turned_ref, total_ref, mine_ref, *, q_len, v_len, lanes,
):
    cap_rows, vid_rows = caps_ref.shape[0], vids_ref.shape[0]
    features = caps_ref.shape[2]
    block_caps = lanes // q_len
    blocks = cap_rows // block_caps
    to_exp2 = 1.0 / (pool_tau * math.log(2.0))

    own_cap = lax.axis_index("x") * lax.axis_size(Z) + lax.axis_index("z_hi") * lax.axis_size("z_lo") + lax.axis_index("z_lo")
    own_vid = lax.axis_index("core") * lax.axis_size("y") + lax.axis_index("y")
    cap_bits = block_caps.bit_length() - 1
    own_block, own_place = own_cap >> cap_bits, own_cap & (block_caps - 1)

    turned_ref[...] = vids_ref[:, :v_len, :].reshape(vid_rows * v_len, features).T
    total_ref[...] = jnp.zeros_like(total_ref)

    def queries_of(block):
        return caps_ref[pl.ds(block * block_caps, block_caps), :q_len, :].reshape(lanes, features)

    @pl.loop(0, blocks)
    def _(block):
        queries = queries_of(block)
        for v in range(vid_rows):
            scores = lax.dot_general(
                vids_ref[v, :v_len, :], queries, (((1,), (1,)), ((), ())), preferred_element_type=jnp.float32
            )
            peak = jnp.max(scores, axis=0, keepdims=True)
            lifted = jnp.exp2((scores - peak) * to_exp2)
            lift_ref[block, v] = lifted
            peak_ref[block, pl.ds(v, 1), :] = peak
            sum_ref[block, pl.ds(v, 1), :] = jnp.sum(lifted, axis=0, keepdims=True)

    q_bits = q_len.bit_length() - 1
    row = lax.broadcasted_iota(jnp.int32, (lanes, lanes), 0) >> q_bits
    col = lax.broadcasted_iota(jnp.int32, (lanes, lanes), 1) >> q_bits
    spread = jnp.where(row == col, 1.0 / (q_len * logit_temp), 0.0)
    col_norm = vids_ref[:, v_len, :1].astype(jnp.float32)
    lane_cap = lax.broadcasted_iota(jnp.int32, (vid_rows, lanes), 1) >> q_bits
    sub_vid = lax.broadcasted_iota(jnp.int32, (vid_rows, lanes), 0)

    mine_ref[...] = jnp.zeros_like(mine_ref)

    @pl.loop(0, blocks)
    def _(block):
        summed = sum_ref[block]
        pooled = peak_ref[block] + pool_tau * jnp.log(summed)
        logits = jnp.dot(pooled, spread, preferred_element_type=jnp.float32, precision=lax.Precision.HIGHEST)
        row_norm = jnp.zeros((1, lanes), jnp.float32)
        for c in range(block_caps):
            norm = caps_ref[block * block_caps + c, pl.ds(q_len, 1), :].astype(jnp.float32)
            norm = jnp.concatenate([norm] * (lanes // norm.shape[1]), axis=1)
            row_norm = jnp.where(lane_cap[:1] == c, norm, row_norm)
        paired = (lane_cap + block * block_caps == own_cap) & (sub_vid == own_vid)
        pair_grad = (jnp.exp(logits - row_norm) + jnp.exp(logits - col_norm) - 2.0 * paired.astype(jnp.float32)) / (2.0 * logit_temp)
        scale = pair_grad / (summed * q_len)
        sum_ref[block] = jnp.where(paired, 0.0, scale)
        mine_ref[...] += jnp.where(paired, scale, 0.0)

    @pl.loop(0, blocks)
    def _(block):
        queries = queries_of(block)
        for v in range(vid_rows):
            coef_ref[pl.ds(v * v_len, v_len), :] = (lift_ref[block, v] * sum_ref[block, pl.ds(v, 1), :]).astype(jnp.bfloat16)
        coef = coef_ref[...]
        turned = jnp.dot(turned_ref[...], coef, preferred_element_type=jnp.float32)
        dq_ref[pl.ds(block * block_caps, block_caps)] = turned.T.reshape(block_caps, q_len, features).astype(dq_ref.dtype)
        total_ref[...] += jnp.dot(coef, queries, preferred_element_type=jnp.float32)

    own_scale = jnp.sum(mine_ref[...], axis=0, keepdims=True)
    coef = (lift_ref[own_block, own_vid] * own_scale).astype(jnp.bfloat16)
    total_ref[pl.ds(own_vid * v_len, v_len), :] += jnp.dot(coef, queries_of(own_block), preferred_element_type=jnp.float32)
    half = vid_rows // 2 * v_len
    core = lax.axis_index("core")
    dv_kept_ref[...] = total_ref[pl.ds(core * half, half), :].reshape(dv_kept_ref.shape)
    dv_sent_ref[...] = total_ref[pl.ds((1 - core) * half, half), :].reshape(dv_sent_ref.shape).astype(dv_sent_ref.dtype)
    total_ref[pl.ds(0, lanes), :] = lax.dot_general(
        coef, vids_ref[own_vid, :v_len, :], (((0,), (0,)), ((), ())), preferred_element_type=jnp.float32
    )
    own_dq_ref[...] = total_ref[pl.ds(own_place * q_len, q_len), :]


def pair_grads(caps, vids, q_len, v_len, lanes=256):
    cap_rows, vid_rows, features = caps.shape[0], vids.shape[0], caps.shape[2]
    blocks = cap_rows * q_len // lanes
    return pl.pallas_call(
        functools.partial(pair_kernel, q_len=q_len, v_len=v_len, lanes=lanes),
        out_shape=(
            jax.ShapeDtypeStruct((cap_rows, q_len, features), jnp.bfloat16),
            jax.ShapeDtypeStruct((q_len, features), jnp.float32),
            jax.ShapeDtypeStruct((vid_rows // 2, v_len, features), jnp.float32),
            jax.ShapeDtypeStruct((vid_rows // 2, v_len, features), jnp.bfloat16),
        ),
        in_specs=[
            pl.BlockSpec(memory_space=pltpu.VMEM),
            pl.BlockSpec(memory_space=pltpu.VMEM),
        ],
        out_specs=[pl.BlockSpec(memory_space=pltpu.VMEM)] * 4,
        scratch_shapes=[
            pltpu.VMEM((blocks, vid_rows, v_len, lanes), jnp.float32),
            pltpu.VMEM((vid_rows * v_len, lanes), jnp.bfloat16),
            pltpu.VMEM((blocks, vid_rows, lanes), jnp.float32),
            pltpu.VMEM((blocks, vid_rows, lanes), jnp.float32),
            pltpu.VMEM((features, vid_rows * v_len), jnp.bfloat16),
            pltpu.VMEM((vid_rows * v_len, features), jnp.float32),
            pltpu.VMEM((vid_rows, lanes), jnp.float32),
        ],
        compiler_params=pltpu.CompilerParams(vmem_limit_bytes=48 * 2**20),
        cost_estimate=pl.CostEstimate(
            flops=6 * cap_rows * q_len * vid_rows * v_len * features,
            bytes_accessed=4 * (cap_rows * q_len + vid_rows * v_len) * features,
            transcendentals=cap_rows * q_len * vid_rows * v_len,
        ),
    )(caps, vids)


PARTS = (2, 8, 4, 8, 2)
AXES = ("z_hi", "y", "x", "z_lo", "core")
Z = ("z_hi", "z_lo")


def with_norm(tokens, norm):
    return jnp.concatenate([tokens, jnp.broadcast_to(norm[:, None, None], (1, 8, tokens.shape[2]))], axis=1)


def spread_over(block, axis):
    size = lax.axis_size(axis)
    copies = jnp.broadcast_to(block[None], (size, *block.shape))
    return lax.all_to_all(copies, axis, 0, 0, tiled=True)


def sum_over(parts, axis):
    moved = lax.all_to_all(parts, axis, 0, 0, tiled=True)
    return jnp.sum(moved.astype(jnp.float32), axis=0)


def halve(kept, sent, axis, bit):
    across = [(i, i ^ (1 << bit)) for i in range(lax.axis_size(axis))]
    return kept + lax.ppermute(sent, axis, across).astype(jnp.float32)


def sum_over_bits(kept, axis):
    bits = lax.axis_size(axis).bit_length() - 1
    for bit in range(bits):
        kept = kept.reshape(-1, 2, *kept.shape[1:])
        own = (lax.axis_index(axis) >> bit) & 1
        sent = lax.dynamic_index_in_dim(kept, 1 - own, 1, keepdims=False)
        kept = lax.dynamic_index_in_dim(kept, own, 1, keepdims=False)
        kept = halve(kept, sent if bit == bits - 1 else sent.astype(jnp.bfloat16), axis, bit)
    return kept[0]


def local(caption_tokens, video_tokens, row_norms, col_norms):
    q_len, v_len, features = caption_tokens.shape[1], video_tokens.shape[1], caption_tokens.shape[2]
    x_count, y_count, z_count = lax.axis_size("x"), lax.axis_size("y"), lax.axis_size(Z)
    caps = spread_over(with_norm(caption_tokens, row_norms)[0], Z)
    vids = lax.all_gather(with_norm(video_tokens, col_norms), "y", axis=0, tiled=True)
    caps, vids = lax.optimization_barrier((caps, vids))
    vids = lax.all_gather(vids, "core", axis=0, tiled=True)
    caps = spread_over(caps, "x").reshape(x_count * z_count, q_len + 8, features)
    dq, own_dq, dv_kept, dv_sent = pair_grads(caps, vids, q_len, v_len)
    dv = sum_over_bits(halve(dv_kept, dv_sent, "core", 0), "y").astype(jnp.bfloat16)
    dq = sum_over(dq.reshape(x_count, z_count, q_len, features), "x").astype(jnp.bfloat16)
    dq = (sum_over(dq, Z) + own_dq).astype(jnp.bfloat16)
    return dq[None], dv[None]


def solution(mesh):
    fine = Mesh(mesh.devices.reshape(PARTS), AXES)
    return jax.shard_map(
        local,
        mesh=fine,
        in_specs=(P(AXES, None, None), P(AXES, None, None), P(AXES), P(AXES)),
        out_specs=(P(AXES, None, None), P(AXES, None, None)),
        check_vma=False,
    )
```

```python
import functools
import math

import jax
import jax.numpy as jnp
from jax import lax
from jax.experimental import pallas as pl
from jax.experimental.pallas import tpu as pltpu
from jax.sharding import Mesh
from jax.sharding import PartitionSpec as P

pool_tau = 0.05
logit_temp = 0.5


def pair_kernel(
    caps_ref, vids_ref, dq_ref, own_dq_ref, dv_kept_ref, dv_sent_ref,
    lift_ref, coef_ref, peak_ref, sum_ref, turned_ref, total_ref, mine_ref, *, q_len, v_len, lanes,
):
    cap_rows, vid_rows = caps_ref.shape[0], vids_ref.shape[0]
    features = caps_ref.shape[2]
    block_caps = lanes // q_len
    blocks = cap_rows // block_caps
    to_exp2 = 1.0 / (pool_tau * math.log(2.0))

    own_cap = lax.axis_index("x") * lax.axis_size(Z) + lax.axis_index("z_hi") * lax.axis_size("z_lo") + lax.axis_index("z_lo")
    own_vid = lax.axis_index("core") * lax.axis_size("y") + lax.axis_index("y")
    cap_bits = block_caps.bit_length() - 1
    own_block, own_place = own_cap >> cap_bits, own_cap & (block_caps - 1)

    turned_ref[...] = vids_ref[:, :v_len, :].reshape(vid_rows * v_len, features).T
    total_ref[...] = jnp.zeros_like(total_ref)

    def queries_of(block):
        return caps_ref[pl.ds(block * block_caps, block_caps), :q_len, :].reshape(lanes, features)

    @pl.loop(0, blocks)
    def _(block):
        queries = queries_of(block)
        for v in range(vid_rows):
            scores = lax.dot_general(
                vids_ref[v, :v_len, :], queries, (((1,), (1,)), ((), ())), preferred_element_type=jnp.float32
            )
            peak = jnp.max(scores, axis=0, keepdims=True)
            lifted = jnp.exp2((scores - peak) * to_exp2)
            lift_ref[block, v] = lifted
            peak_ref[block, pl.ds(v, 1), :] = peak
            sum_ref[block, pl.ds(v, 1), :] = jnp.sum(lifted, axis=0, keepdims=True)

    q_bits = q_len.bit_length() - 1
    row = lax.broadcasted_iota(jnp.int32, (lanes, lanes), 0) >> q_bits
    col = lax.broadcasted_iota(jnp.int32, (lanes, lanes), 1) >> q_bits
    spread = jnp.where(row == col, 1.0 / (q_len * logit_temp), 0.0)
    col_norm = vids_ref[:, v_len, :1].astype(jnp.float32)
    lane_cap = lax.broadcasted_iota(jnp.int32, (vid_rows, lanes), 1) >> q_bits
    sub_vid = lax.broadcasted_iota(jnp.int32, (vid_rows, lanes), 0)

    mine_ref[...] = jnp.zeros_like(mine_ref)

    @pl.loop(0, blocks)
    def _(block):
        summed = sum_ref[block]
        pooled = peak_ref[block] + pool_tau * jnp.log(summed)
        logits = jnp.dot(pooled, spread, preferred_element_type=jnp.float32, precision=lax.Precision.HIGHEST)
        row_norm = jnp.zeros((1, lanes), jnp.float32)
        for c in range(block_caps):
            norm = caps_ref[block * block_caps + c, pl.ds(q_len, 1), :].astype(jnp.float32)
            norm = jnp.concatenate([norm] * (lanes // norm.shape[1]), axis=1)
            row_norm = jnp.where(lane_cap[:1] == c, norm, row_norm)
        paired = (lane_cap + block * block_caps == own_cap) & (sub_vid == own_vid)
        pair_grad = (jnp.exp(logits - row_norm) + jnp.exp(logits - col_norm) - 2.0 * paired.astype(jnp.float32)) / (2.0 * logit_temp)
        scale = pair_grad / (summed * q_len)
        sum_ref[block] = jnp.where(paired, 0.0, scale)
        mine_ref[...] += jnp.where(paired, scale, 0.0)

    @pl.loop(0, blocks)
    def _(block):
        queries = queries_of(block)
        for v in range(vid_rows):
            coef_ref[pl.ds(v * v_len, v_len), :] = (lift_ref[block, v] * sum_ref[block, pl.ds(v, 1), :]).astype(jnp.bfloat16)
        coef = coef_ref[...]
        turned = jnp.dot(turned_ref[...], coef, preferred_element_type=jnp.float32)
        dq_ref[pl.ds(block * block_caps, block_caps)] = turned.T.reshape(block_caps, q_len, features).astype(dq_ref.dtype)
        total_ref[...] += jnp.dot(coef, queries, preferred_element_type=jnp.float32)

    own_scale = jnp.sum(mine_ref[...], axis=0, keepdims=True)
    coef = (lift_ref[own_block, own_vid] * own_scale).astype(jnp.bfloat16)
    total_ref[pl.ds(own_vid * v_len, v_len), :] += jnp.dot(coef, queries_of(own_block), preferred_element_type=jnp.float32)
    half = vid_rows // 2 * v_len
    core = lax.axis_index("core")
    dv_kept_ref[...] = total_ref[pl.ds(core * half, half), :].reshape(dv_kept_ref.shape)
    dv_sent_ref[...] = total_ref[pl.ds((1 - core) * half, half), :].reshape(dv_sent_ref.shape).astype(dv_sent_ref.dtype)
    total_ref[pl.ds(0, lanes), :] = lax.dot_general(
        coef, vids_ref[own_vid, :v_len, :], (((0,), (0,)), ((), ())), preferred_element_type=jnp.float32
    )
    own_dq_ref[...] = total_ref[pl.ds(own_place * q_len, q_len), :]


def pair_grads(caps, vids, q_len, v_len, lanes=256):
    cap_rows, vid_rows, features = caps.shape[0], vids.shape[0], caps.shape[2]
    blocks = cap_rows * q_len // lanes
    return pl.pallas_call(
        functools.partial(pair_kernel, q_len=q_len, v_len=v_len, lanes=lanes),
        out_shape=(
            jax.ShapeDtypeStruct((cap_rows, q_len, features), jnp.bfloat16),
            jax.ShapeDtypeStruct((q_len, features), jnp.float32),
            jax.ShapeDtypeStruct((vid_rows // 2, v_len, features), jnp.float32),
            jax.ShapeDtypeStruct((vid_rows // 2, v_len, features), jnp.bfloat16),
        ),
        in_specs=[
            pl.BlockSpec(memory_space=pltpu.VMEM),
            pl.BlockSpec(memory_space=pltpu.VMEM),
        ],
        out_specs=[pl.BlockSpec(memory_space=pltpu.VMEM)] * 4,
        scratch_shapes=[
            pltpu.VMEM((blocks, vid_rows, v_len, lanes), jnp.float32),
            pltpu.VMEM((vid_rows * v_len, lanes), jnp.bfloat16),
            pltpu.VMEM((blocks, vid_rows, lanes), jnp.float32),
            pltpu.VMEM((blocks, vid_rows, lanes), jnp.float32),
            pltpu.VMEM((features, vid_rows * v_len), jnp.bfloat16),
            pltpu.VMEM((vid_rows * v_len, features), jnp.float32),
            pltpu.VMEM((vid_rows, lanes), jnp.float32),
        ],
        compiler_params=pltpu.CompilerParams(vmem_limit_bytes=48 * 2**20),
        cost_estimate=pl.CostEstimate(
            flops=6 * cap_rows * q_len * vid_rows * v_len * features,
            bytes_accessed=4 * (cap_rows * q_len + vid_rows * v_len) * features,
            transcendentals=cap_rows * q_len * vid_rows * v_len,
        ),
    )(caps, vids)


PARTS = (2, 8, 4, 8, 2)
AXES = ("z_hi", "y", "x", "z_lo", "core")
Z = ("z_hi", "z_lo")


def with_norm(tokens, norm):
    return jnp.concatenate([tokens, jnp.broadcast_to(norm[:, None, None], (1, 8, tokens.shape[2]))], axis=1)


def spread_over(block, axis):
    size = lax.axis_size(axis)
    copies = jnp.broadcast_to(block[None], (size, *block.shape))
    return lax.all_to_all(copies, axis, 0, 0, tiled=True)


def sum_over(parts, axis):
    moved = lax.all_to_all(parts, axis, 0, 0, tiled=True)
    return jnp.sum(moved.astype(jnp.float32), axis=0)


def local(caption_tokens, video_tokens, row_norms, col_norms):
    q_len, v_len, features = caption_tokens.shape[1], video_tokens.shape[1], caption_tokens.shape[2]
    x_count, z_count = lax.axis_size("x"), lax.axis_size(Z)
    caps = spread_over(with_norm(caption_tokens, row_norms)[0], Z)
    vids = with_norm(video_tokens, col_norms)
    caps, vids = lax.optimization_barrier((caps, vids))
    vids = spread_over(vids[0], "y")
    caps = lax.all_gather(caps, "x", axis=0, tiled=True)
    vids = lax.all_gather(vids, "core", axis=0, tiled=True)
    dq, own_dq, dv_kept, dv_sent = pair_grads(caps, vids, q_len, v_len)
    dv = dv_kept + lax.ppermute(dv_sent, "core", [(0, 1), (1, 0)]).astype(jnp.float32)
    dv = lax.psum_scatter(dv, "y", scatter_dimension=0, tiled=False).astype(jnp.bfloat16)
    dq = sum_over(dq.reshape(x_count, z_count, q_len, features), "x").astype(jnp.bfloat16)
    dq = (sum_over(dq, Z) + own_dq).astype(jnp.bfloat16)
    return dq[None], dv[None]


def solution(mesh):
    fine = Mesh(mesh.devices.reshape(PARTS), AXES)
    return jax.shard_map(
        local,
        mesh=fine,
        in_specs=(P(AXES, None, None), P(AXES, None, None), P(AXES), P(AXES)),
        out_specs=(P(AXES, None, None), P(AXES, None, None)),
        check_vma=False,
    )
```

```python
import functools
import math

import jax
import jax.numpy as jnp
from jax import lax
from jax.experimental import pallas as pl
from jax.experimental.pallas import tpu as pltpu
from jax.sharding import Mesh
from jax.sharding import PartitionSpec as P

pool_tau = 0.05
logit_temp = 0.5


def block_queries(caps_ref, block, lanes, q_len):
    block_caps = lanes // q_len
    return caps_ref[pl.ds(block * block_caps, block_caps), :q_len, :].reshape(lanes, caps_ref.shape[2])


def video_kernel(
    caps_ref, vids_ref, kept_ref, sent_ref, turned_ref, out_ref,
    lift_ref, peak_ref, sum_ref, total_ref, coef_ref, done, *, q_len, v_len, lanes,
):
    cap_rows, vid_rows = caps_ref.shape[0], vids_ref.shape[0]
    features = caps_ref.shape[2]
    block_caps = lanes // q_len
    blocks = cap_rows // block_caps
    to_exp2 = 1.0 / (pool_tau * math.log(2.0))

    own_cap = lax.axis_index("x") * lax.axis_size(Z) + lax.axis_index("z_hi") * lax.axis_size("z_lo") + lax.axis_index("z_lo")
    own_vid = lax.axis_index("core") * lax.axis_size("y") + lax.axis_index("y")

    turned_ref[...] = vids_ref[:, :v_len, :].reshape(vid_rows * v_len, features).T
    total_ref[...] = jnp.zeros_like(total_ref)

    @pl.loop(0, blocks)
    def _(block):
        queries = block_queries(caps_ref, block, lanes, q_len)
        for v in range(vid_rows):
            scores = lax.dot_general(
                vids_ref[v, :v_len, :], queries, (((1,), (1,)), ((), ())), preferred_element_type=jnp.float32
            )
            peak = jnp.max(scores, axis=0, keepdims=True)
            lifted = jnp.exp2((scores - peak) * to_exp2)
            lift_ref[block, v] = lifted
            peak_ref[block, pl.ds(v, 1), :] = peak
            sum_ref[block, pl.ds(v, 1), :] = jnp.sum(lifted, axis=0, keepdims=True)

    q_bits = q_len.bit_length() - 1
    row = lax.broadcasted_iota(jnp.int32, (lanes, lanes), 0) >> q_bits
    col = lax.broadcasted_iota(jnp.int32, (lanes, lanes), 1) >> q_bits
    spread = jnp.where(row == col, 1.0 / (q_len * logit_temp), 0.0)
    col_norm = vids_ref[:, v_len, :1].astype(jnp.float32)
    lane_cap = lax.broadcasted_iota(jnp.int32, (vid_rows, lanes), 1) >> q_bits
    sub_vid = lax.broadcasted_iota(jnp.int32, (vid_rows, lanes), 0)

    for block in range(blocks):
        summed = sum_ref[block]
        pooled = peak_ref[block] + pool_tau * jnp.log(summed)
        logits = jnp.dot(pooled, spread, preferred_element_type=jnp.float32, precision=lax.Precision.HIGHEST)
        row_norm = jnp.zeros((1, lanes), jnp.float32)
        for c in range(block_caps):
            norm = caps_ref[block * block_caps + c, pl.ds(q_len, 1), :].astype(jnp.float32)
            norm = jnp.concatenate([norm] * (lanes // norm.shape[1]), axis=1)
            row_norm = jnp.where(lane_cap[:1] == c, norm, row_norm)
        paired = (lane_cap + block * block_caps == own_cap) & (sub_vid == own_vid)
        pair_grad = (jnp.exp(logits - row_norm) + jnp.exp(logits - col_norm) - 2.0 * paired.astype(jnp.float32)) / (2.0 * logit_temp)
        sum_ref[block] = pair_grad / (summed * q_len)

    @pl.loop(0, blocks)
    def _(block):
        for v in range(vid_rows):
            coef_ref[block, pl.ds(v * v_len, v_len), :] = (lift_ref[block, v] * sum_ref[block, pl.ds(v, 1), :]).astype(jnp.bfloat16)
        pltpu.make_async_copy(coef_ref.at[block], out_ref.at[block], done.at[block]).start()
        total_ref[...] += jnp.dot(coef_ref[block], block_queries(caps_ref, block, lanes, q_len), preferred_element_type=jnp.float32)

    half = vid_rows // 2 * v_len
    core = lax.axis_index("core")
    kept_ref[...] = total_ref[pl.ds(core * half, half), :].reshape(kept_ref.shape)
    sent_ref[...] = total_ref[pl.ds((1 - core) * half, half), :].reshape(sent_ref.shape).astype(sent_ref.dtype)
    for block in range(blocks):
        pltpu.make_async_copy(coef_ref.at[block], out_ref.at[block], done.at[block]).wait()


def caption_kernel(in_ref, turned_ref, *refs):
    *sum_refs, coef_ref, done = refs
    x_count = len(sum_refs)
    x_blocks = coef_ref.shape[0] // x_count
    lanes, features = coef_ref.shape[2], turned_ref.shape[0]
    q_len = sum_refs[0].shape[1]
    block_caps = lanes // q_len

    def copy(away, part):
        place, slot = lax.rem(lax.axis_index("x") + away, x_count), away * x_blocks + part
        return pltpu.make_async_copy(in_ref.at[place * x_blocks + part], coef_ref.at[slot], done.at[slot])

    for away in range(x_count):
        for part in range(x_blocks):
            copy(away, part).start()
    for away, ref in enumerate(sum_refs):
        for part in range(x_blocks):
            copy(away, part).wait()
            turned = jnp.dot(turned_ref[...], coef_ref[away * x_blocks + part], preferred_element_type=jnp.float32)
            ref[pl.ds(part * block_caps, block_caps)] = turned.T.reshape(block_caps, q_len, features).astype(ref.dtype)


def video_grads(caps, vids, q_len, v_len, lanes=256):
    cap_rows, vid_rows, features = caps.shape[0], vids.shape[0], caps.shape[2]
    blocks = cap_rows * q_len // lanes
    pairs = cap_rows * q_len * vid_rows * v_len
    return pl.pallas_call(
        functools.partial(video_kernel, q_len=q_len, v_len=v_len, lanes=lanes),
        out_shape=(
            jax.ShapeDtypeStruct((vid_rows // 2, v_len, features), jnp.float32),
            jax.ShapeDtypeStruct((vid_rows // 2, v_len, features), jnp.bfloat16),
            jax.ShapeDtypeStruct((features, vid_rows * v_len), jnp.bfloat16),
            jax.ShapeDtypeStruct((blocks, vid_rows * v_len, lanes), jnp.bfloat16),
        ),
        in_specs=[pl.BlockSpec(memory_space=pltpu.VMEM)] * 2,
        out_specs=[pl.BlockSpec(memory_space=pltpu.VMEM)] * 3 + [pl.BlockSpec(memory_space=pl.ANY)],
        scratch_shapes=[
            pltpu.VMEM((blocks, vid_rows, v_len, lanes), jnp.float32),
            pltpu.VMEM((blocks, vid_rows, lanes), jnp.float32),
            pltpu.VMEM((blocks, vid_rows, lanes), jnp.float32),
            pltpu.VMEM((vid_rows * v_len, features), jnp.float32),
            pltpu.VMEM((blocks, vid_rows * v_len, lanes), jnp.bfloat16),
            pltpu.SemaphoreType.DMA((blocks,)),
        ],
        compiler_params=pltpu.CompilerParams(vmem_limit_bytes=51 * 2**20),
        cost_estimate=pl.CostEstimate(flops=4 * pairs * features, bytes_accessed=2 * pairs, transcendentals=pairs),
    )(caps, vids)


def caption_grads(coef, turned, x_count, z_count, q_len):
    features = turned.shape[0]
    return pl.pallas_call(
        caption_kernel,
        out_shape=tuple(
            jax.ShapeDtypeStruct((z_count, q_len, features), jnp.bfloat16 if away else jnp.float32) for away in range(x_count)
        ),
        in_specs=[pl.BlockSpec(memory_space=pl.ANY), pl.BlockSpec(memory_space=pltpu.VMEM)],
        out_specs=[pl.BlockSpec(memory_space=pltpu.VMEM)] * x_count,
        scratch_shapes=[pltpu.VMEM(coef.shape, coef.dtype), pltpu.SemaphoreType.DMA((coef.shape[0],))],
        compiler_params=pltpu.CompilerParams(vmem_limit_bytes=51 * 2**20),
        cost_estimate=pl.CostEstimate(flops=2 * coef.size * features, bytes_accessed=2 * coef.size, transcendentals=0),
    )(coef, turned)


PARTS = (2, 8, 4, 8, 2)
AXES = ("z_hi", "y", "x", "z_lo", "core")
Z = ("z_hi", "z_lo")


def with_norm(tokens, norm):
    return jnp.concatenate([tokens, jnp.broadcast_to(norm[:, None, None], (1, 8, tokens.shape[2]))], axis=1)


def spread_over(block, axis):
    size = lax.axis_size(axis)
    copies = jnp.broadcast_to(block[None], (size, *block.shape))
    return lax.all_to_all(copies, axis, 0, 0, tiled=True)


def send(sums, axis):
    return lax.all_to_all(sums.astype(jnp.bfloat16), axis, 0, 0, tiled=True)


def add_up(sums, moved, axis):
    place = lax.axis_index(axis)
    others = lax.broadcasted_iota(jnp.int32, sums.shape, 0) != place
    own = lax.dynamic_index_in_dim(sums, place, 0, keepdims=False)
    return (jnp.sum(jnp.where(others, moved.astype(jnp.float32), 0.0), axis=0) + own).astype(jnp.bfloat16)


def local(caption_tokens, video_tokens, row_norms, col_norms):
    q_len, v_len, features = caption_tokens.shape[1], video_tokens.shape[1], caption_tokens.shape[2]
    x_count, z_count = lax.axis_size("x"), lax.axis_size(Z)
    caps = spread_over(with_norm(caption_tokens, row_norms)[0], Z)
    vids = with_norm(video_tokens, col_norms)
    caps, vids = lax.optimization_barrier((caps, vids))
    vids = spread_over(vids[0], "y")
    caps = lax.all_gather(caps, "x", axis=0, tiled=True)
    vids = lax.all_gather(vids, "core", axis=0, tiled=True)
    dv, dv_sent, turned, coef = video_grads(caps, vids, q_len, v_len)
    dv = dv + lax.ppermute(dv_sent, "core", [(0, 1), (1, 0)]).astype(jnp.float32)
    dv, turned = lax.optimization_barrier((dv, turned))
    dv_moved = send(dv, "y")
    dq, *dq_sent = caption_grads(coef, turned, x_count, z_count, q_len)
    for away, sent in enumerate(dq_sent, 1):
        dq = dq + lax.ppermute(sent, "x", [(i, (i + away) % x_count) for i in range(x_count)]).astype(jnp.float32)
    dq, dv_moved = lax.optimization_barrier((dq, dv_moved))
    return add_up(dq, send(dq, Z), Z)[None], add_up(dv, dv_moved, "y")[None]


def solution(mesh):
    fine = Mesh(mesh.devices.reshape(PARTS), AXES)
    return jax.shard_map(
        local,
        mesh=fine,
        in_specs=(P(AXES, None, None), P(AXES, None, None), P(AXES), P(AXES)),
        out_specs=(P(AXES, None, None), P(AXES, None, None)),
        check_vma=False,
    )
```

```python
import functools
import math

import jax
import jax.numpy as jnp
from jax import lax
from jax.experimental import pallas as pl
from jax.experimental.pallas import tpu as pltpu
from jax.sharding import Mesh
from jax.sharding import PartitionSpec as P

pool_tau = 0.05
logit_temp = 0.5


def pair_kernel(
    caps_ref, vids_ref, dq_ref, own_dq_ref, dv_kept_ref, dv_sent_ref,
    lift_ref, coef_ref, peak_ref, sum_ref, turned_ref, total_ref, mine_ref, *, q_len, v_len, lanes,
):
    cap_rows, vid_rows = caps_ref.shape[0], vids_ref.shape[0]
    features = caps_ref.shape[2]
    block_caps = lanes // q_len
    blocks = cap_rows // block_caps
    to_exp2 = 1.0 / (pool_tau * math.log(2.0))

    own_cap = lax.axis_index("x") * lax.axis_size(Z) + lax.axis_index("z_hi") * lax.axis_size("z_lo") + lax.axis_index("z_lo")
    own_vid = lax.axis_index("core") * lax.axis_size("y") + lax.axis_index("y")
    cap_bits = block_caps.bit_length() - 1
    own_block, own_place = own_cap >> cap_bits, own_cap & (block_caps - 1)

    turned_ref[...] = vids_ref[:, :v_len, :].reshape(vid_rows * v_len, features).T
    total_ref[...] = jnp.zeros_like(total_ref)

    def queries_of(block):
        return caps_ref[pl.ds(block * block_caps, block_caps), :q_len, :].reshape(lanes, features)

    def score(block):
        queries = queries_of(block)
        for v in range(vid_rows):
            scores = lax.dot_general(
                vids_ref[v, :v_len, :], queries, (((1,), (1,)), ((), ())), preferred_element_type=jnp.float32
            )
            peak = jnp.max(scores, axis=0, keepdims=True)
            lifted = jnp.exp2((scores - peak) * to_exp2)
            lift_ref[block, v] = lifted
            peak_ref[block, pl.ds(v, 1), :] = peak
            sum_ref[block, pl.ds(v, 1), :] = jnp.sum(lifted, axis=0, keepdims=True)

    q_bits = q_len.bit_length() - 1
    row = lax.broadcasted_iota(jnp.int32, (lanes, lanes), 0) >> q_bits
    col = lax.broadcasted_iota(jnp.int32, (lanes, lanes), 1) >> q_bits
    spread = jnp.where(row == col, 1.0 / (q_len * logit_temp), 0.0)
    col_norm = vids_ref[:, v_len, :1].astype(jnp.float32)
    lane_cap = lax.broadcasted_iota(jnp.int32, (vid_rows, lanes), 1) >> q_bits
    sub_vid = lax.broadcasted_iota(jnp.int32, (vid_rows, lanes), 0)

    mine_ref[...] = jnp.zeros_like(mine_ref)

    def scale(block):
        summed = sum_ref[block]
        pooled = peak_ref[block] + pool_tau * jnp.log(summed)
        logits = jnp.dot(pooled, spread, preferred_element_type=jnp.float32, precision=lax.Precision.HIGHEST)
        row_norm = jnp.zeros((1, lanes), jnp.float32)
        for c in range(block_caps):
            norm = caps_ref[block * block_caps + c, pl.ds(q_len, 1), :].astype(jnp.float32)
            norm = jnp.concatenate([norm] * (lanes // norm.shape[1]), axis=1)
            row_norm = jnp.where(lane_cap[:1] == c, norm, row_norm)
        paired = (lane_cap + block * block_caps == own_cap) & (sub_vid == own_vid)
        pair_grad = (jnp.exp(logits - row_norm) + jnp.exp(logits - col_norm) - 2.0 * paired.astype(jnp.float32)) / (2.0 * logit_temp)
        factor = pair_grad / (summed * q_len)
        sum_ref[block] = jnp.where(paired, 0.0, factor)
        mine_ref[...] += jnp.where(paired, factor, 0.0)

    def multiply(block):
        queries = queries_of(block)
        for v in range(vid_rows):
            coef_ref[pl.ds(v * v_len, v_len), :] = (lift_ref[block, v] * sum_ref[block, pl.ds(v, 1), :]).astype(jnp.bfloat16)
        coef = coef_ref[...]
        turned = jnp.dot(turned_ref[...], coef, preferred_element_type=jnp.float32)
        dq_ref[pl.ds(block * block_caps, block_caps)] = turned.T.reshape(block_caps, q_len, features).astype(dq_ref.dtype)
        total_ref[...] += jnp.dot(coef, queries, preferred_element_type=jnp.float32)

    score(0)
    scale(0)
    for block in range(1, blocks):
        score(block)
        multiply(block - 1)
        scale(block)
    multiply(blocks - 1)

    own_scale = jnp.sum(mine_ref[...], axis=0, keepdims=True)
    coef = (lift_ref[own_block, own_vid] * own_scale).astype(jnp.bfloat16)
    total_ref[pl.ds(own_vid * v_len, v_len), :] += jnp.dot(coef, queries_of(own_block), preferred_element_type=jnp.float32)
    half = vid_rows // 2 * v_len
    core = lax.axis_index("core")
    dv_kept_ref[...] = total_ref[pl.ds(core * half, half), :].reshape(dv_kept_ref.shape)
    dv_sent_ref[...] = total_ref[pl.ds((1 - core) * half, half), :].reshape(dv_sent_ref.shape).astype(dv_sent_ref.dtype)
    total_ref[pl.ds(0, lanes), :] = lax.dot_general(
        coef, vids_ref[own_vid, :v_len, :], (((0,), (0,)), ((), ())), preferred_element_type=jnp.float32
    )
    own_dq_ref[...] = total_ref[pl.ds(own_place * q_len, q_len), :]


def pair_grads(caps, vids, q_len, v_len, lanes=256):
    cap_rows, vid_rows, features = caps.shape[0], vids.shape[0], caps.shape[2]
    blocks = cap_rows * q_len // lanes
    return pl.pallas_call(
        functools.partial(pair_kernel, q_len=q_len, v_len=v_len, lanes=lanes),
        out_shape=(
            jax.ShapeDtypeStruct((cap_rows, q_len, features), jnp.bfloat16),
            jax.ShapeDtypeStruct((q_len, features), jnp.float32),
            jax.ShapeDtypeStruct((vid_rows // 2, v_len, features), jnp.float32),
            jax.ShapeDtypeStruct((vid_rows // 2, v_len, features), jnp.bfloat16),
        ),
        in_specs=[
            pl.BlockSpec(memory_space=pltpu.VMEM),
            pl.BlockSpec(memory_space=pltpu.VMEM),
        ],
        out_specs=[pl.BlockSpec(memory_space=pltpu.VMEM)] * 4,
        scratch_shapes=[
            pltpu.VMEM((blocks, vid_rows, v_len, lanes), jnp.float32),
            pltpu.VMEM((vid_rows * v_len, lanes), jnp.bfloat16),
            pltpu.VMEM((blocks, vid_rows, lanes), jnp.float32),
            pltpu.VMEM((blocks, vid_rows, lanes), jnp.float32),
            pltpu.VMEM((features, vid_rows * v_len), jnp.bfloat16),
            pltpu.VMEM((vid_rows * v_len, features), jnp.float32),
            pltpu.VMEM((vid_rows, lanes), jnp.float32),
        ],
        compiler_params=pltpu.CompilerParams(vmem_limit_bytes=48 * 2**20),
        cost_estimate=pl.CostEstimate(
            flops=6 * cap_rows * q_len * vid_rows * v_len * features,
            bytes_accessed=4 * (cap_rows * q_len + vid_rows * v_len) * features,
            transcendentals=cap_rows * q_len * vid_rows * v_len,
        ),
    )(caps, vids)


PARTS = (2, 8, 4, 8, 2)
AXES = ("z_hi", "y", "x", "z_lo", "core")
Z = ("z_hi", "z_lo")


def with_norm(tokens, norm):
    return jnp.concatenate([tokens, jnp.broadcast_to(norm[:, None, None], (1, 8, tokens.shape[2]))], axis=1)


def spread_over(block, axis):
    size = lax.axis_size(axis)
    copies = jnp.broadcast_to(block[None], (size, *block.shape))
    return lax.all_to_all(copies, axis, 0, 0, tiled=True)


def sum_over(parts, axis):
    moved = lax.all_to_all(parts, axis, 0, 0, tiled=True)
    return jnp.sum(moved.astype(jnp.float32), axis=0)


def halve(kept, sent, axis, bit):
    across = [(i, i ^ (1 << bit)) for i in range(lax.axis_size(axis))]
    return kept + lax.ppermute(sent, axis, across).astype(jnp.float32)


def sum_over_bit(kept, axis, bit, dtype):
    kept = kept.reshape(-1, 2, *kept.shape[1:])
    own = (lax.axis_index(axis) >> bit) & 1
    sent = lax.dynamic_index_in_dim(kept, 1 - own, 1, keepdims=False).astype(dtype)
    return halve(lax.dynamic_index_in_dim(kept, own, 1, keepdims=False), sent, axis, bit)


def local(caption_tokens, video_tokens, row_norms, col_norms):
    q_len, v_len, features = caption_tokens.shape[1], video_tokens.shape[1], caption_tokens.shape[2]
    x_count, z_count = lax.axis_size("x"), lax.axis_size(Z)
    caps = spread_over(with_norm(caption_tokens, row_norms)[0], Z)
    vids = with_norm(video_tokens, col_norms)
    caps, vids = lax.optimization_barrier((caps, vids))
    vids = spread_over(vids[0], "y")
    caps = lax.all_gather(caps, "x", axis=0, tiled=True)
    vids = lax.all_gather(vids, "core", axis=0, tiled=True)
    dq, own_dq, dv_kept, dv_sent = pair_grads(caps, vids, q_len, v_len)
    dq = sum_over(dq.reshape(x_count, z_count, q_len, features), "x").astype(jnp.bfloat16)
    dv = halve(dv_kept, dv_sent, "core", 0)
    last = lax.axis_size("y").bit_length() - 2
    for bit in range(last):
        dv = sum_over_bit(dv, "y", bit, jnp.bfloat16)
    dq, dv = lax.optimization_barrier((dq, dv))
    dv = sum_over_bit(dv, "y", last, jnp.float32)[0].astype(jnp.bfloat16)
    dq = (sum_over(dq, Z) + own_dq).astype(jnp.bfloat16)
    return dq[None], dv[None]


def solution(mesh):
    fine = Mesh(mesh.devices.reshape(PARTS), AXES)
    return jax.shard_map(
        local,
        mesh=fine,
        in_specs=(P(AXES, None, None), P(AXES, None, None), P(AXES), P(AXES)),
        out_specs=(P(AXES, None, None), P(AXES, None, None)),
        check_vma=False,
    )
```

```python
import functools
import math

import jax
import jax.numpy as jnp
from jax import lax
from jax.experimental import pallas as pl
from jax.experimental.pallas import tpu as pltpu
from jax.sharding import Mesh
from jax.sharding import PartitionSpec as P

pool_tau = 0.05
logit_temp = 0.5


def pair_kernel(
    caps_ref, vids_ref, dq_ref, own_dq_ref, dv_kept_ref, dv_sent_ref,
    lift_ref, coef_ref, peak_ref, sum_ref, turned_ref, total_ref, mine_ref, *, q_len, v_len, lanes,
):
    cap_rows, vid_rows = caps_ref.shape[0], vids_ref.shape[0]
    features = caps_ref.shape[2]
    block_caps = lanes // q_len
    blocks = cap_rows // block_caps
    to_exp2 = 1.0 / (pool_tau * math.log(2.0))

    own_cap = lax.axis_index("x") * lax.axis_size(Z) + lax.axis_index("z_hi") * lax.axis_size("z_lo") + lax.axis_index("z_lo")
    own_vid = lax.axis_index("y") * lax.axis_size("core") + lax.axis_index("core")
    cap_bits = block_caps.bit_length() - 1
    own_block, own_place = own_cap >> cap_bits, own_cap & (block_caps - 1)

    turned_ref[...] = vids_ref[:, :v_len, :].reshape(vid_rows * v_len, features).T
    total_ref[...] = jnp.zeros_like(total_ref)

    def queries_of(block):
        return caps_ref[pl.ds(block * block_caps, block_caps), :q_len, :].reshape(lanes, features)

    def score(block):
        queries = queries_of(block)
        for v in range(vid_rows):
            scores = lax.dot_general(
                vids_ref[v, :v_len, :], queries, (((1,), (1,)), ((), ())), preferred_element_type=jnp.float32
            )
            peak = jnp.max(scores, axis=0, keepdims=True)
            lifted = jnp.exp2((scores - peak) * to_exp2)
            lift_ref[block, v] = lifted
            peak_ref[block, pl.ds(v, 1), :] = peak
            sum_ref[block, pl.ds(v, 1), :] = jnp.sum(lifted, axis=0, keepdims=True)

    q_bits = q_len.bit_length() - 1
    row = lax.broadcasted_iota(jnp.int32, (lanes, lanes), 0) >> q_bits
    col = lax.broadcasted_iota(jnp.int32, (lanes, lanes), 1) >> q_bits
    spread = jnp.where(row == col, 1.0 / (q_len * logit_temp), 0.0)
    col_norm = vids_ref[:, v_len, :1].astype(jnp.float32)
    lane_cap = lax.broadcasted_iota(jnp.int32, (vid_rows, lanes), 1) >> q_bits
    sub_vid = lax.broadcasted_iota(jnp.int32, (vid_rows, lanes), 0)

    mine_ref[...] = jnp.zeros_like(mine_ref)

    def scale(block):
        summed = sum_ref[block]
        pooled = peak_ref[block] + pool_tau * jnp.log(summed)
        logits = jnp.dot(pooled, spread, preferred_element_type=jnp.float32, precision=lax.Precision.HIGHEST)
        row_norm = jnp.zeros((1, lanes), jnp.float32)
        for c in range(block_caps):
            norm = caps_ref[block * block_caps + c, pl.ds(q_len, 1), :].astype(jnp.float32)
            norm = jnp.concatenate([norm] * (lanes // norm.shape[1]), axis=1)
            row_norm = jnp.where(lane_cap[:1] == c, norm, row_norm)
        paired = (lane_cap + block * block_caps == own_cap) & (sub_vid == own_vid)
        pair_grad = (jnp.exp(logits - row_norm) + jnp.exp(logits - col_norm) - 2.0 * paired.astype(jnp.float32)) / (2.0 * logit_temp)
        factor = pair_grad / (summed * q_len)
        sum_ref[block] = jnp.where(paired, 0.0, factor)
        mine_ref[...] += jnp.where(paired, factor, 0.0)

    def multiply(block):
        queries = queries_of(block)
        for v in range(vid_rows):
            coef_ref[pl.ds(v * v_len, v_len), :] = (lift_ref[block, v] * sum_ref[block, pl.ds(v, 1), :]).astype(jnp.bfloat16)
        coef = coef_ref[...]
        turned = jnp.dot(turned_ref[...], coef, preferred_element_type=jnp.float32)
        dq_ref[pl.ds(block * block_caps, block_caps)] = turned.T.reshape(block_caps, q_len, features).astype(dq_ref.dtype)
        total_ref[...] += jnp.dot(coef, queries, preferred_element_type=jnp.float32)

    score(0)
    scale(0)
    for block in range(1, blocks):
        score(block)
        multiply(block - 1)
        scale(block)
    multiply(blocks - 1)

    own_scale = jnp.sum(mine_ref[...], axis=0, keepdims=True)
    coef = (lift_ref[own_block, own_vid] * own_scale).astype(jnp.bfloat16)
    total_ref[pl.ds(own_vid * v_len, v_len), :] += jnp.dot(coef, queries_of(own_block), preferred_element_type=jnp.float32)
    bit = lax.axis_index("y") & 1
    y_half = lax.axis_size("y") // 2
    for pair in range(vid_rows // 2):
        core, high = divmod(pair, y_half)
        kept_at, sent_at = (4 * high + 2 * bit + core) * v_len, (4 * high + 2 - 2 * bit + core) * v_len
        dv_kept_ref[pair] = total_ref[pl.ds(pl.multiple_of(kept_at, v_len), v_len), :]
        dv_sent_ref[pair] = total_ref[pl.ds(pl.multiple_of(sent_at, v_len), v_len), :].astype(dv_sent_ref.dtype)
    total_ref[pl.ds(0, lanes), :] = lax.dot_general(
        coef, vids_ref[own_vid, :v_len, :], (((0,), (0,)), ((), ())), preferred_element_type=jnp.float32
    )
    own_dq_ref[...] = total_ref[pl.ds(own_place * q_len, q_len), :]


def pair_grads(caps, vids, q_len, v_len, lanes=256):
    cap_rows, vid_rows, features = caps.shape[0], vids.shape[0], caps.shape[2]
    blocks = cap_rows * q_len // lanes
    return pl.pallas_call(
        functools.partial(pair_kernel, q_len=q_len, v_len=v_len, lanes=lanes),
        out_shape=(
            jax.ShapeDtypeStruct((cap_rows, q_len, features), jnp.bfloat16),
            jax.ShapeDtypeStruct((q_len, features), jnp.float32),
            jax.ShapeDtypeStruct((vid_rows // 2, v_len, features), jnp.float32),
            jax.ShapeDtypeStruct((vid_rows // 2, v_len, features), jnp.bfloat16),
        ),
        in_specs=[
            pl.BlockSpec(memory_space=pltpu.VMEM),
            pl.BlockSpec(memory_space=pltpu.VMEM),
        ],
        out_specs=[pl.BlockSpec(memory_space=pltpu.VMEM)] * 4,
        scratch_shapes=[
            pltpu.VMEM((blocks, vid_rows, v_len, lanes), jnp.float32),
            pltpu.VMEM((vid_rows * v_len, lanes), jnp.bfloat16),
            pltpu.VMEM((blocks, vid_rows, lanes), jnp.float32),
            pltpu.VMEM((blocks, vid_rows, lanes), jnp.float32),
            pltpu.VMEM((features, vid_rows * v_len), jnp.bfloat16),
            pltpu.VMEM((vid_rows * v_len, features), jnp.float32),
            pltpu.VMEM((vid_rows, lanes), jnp.float32),
        ],
        compiler_params=pltpu.CompilerParams(vmem_limit_bytes=48 * 2**20),
        cost_estimate=pl.CostEstimate(
            flops=6 * cap_rows * q_len * vid_rows * v_len * features,
            bytes_accessed=4 * (cap_rows * q_len + vid_rows * v_len) * features,
            transcendentals=cap_rows * q_len * vid_rows * v_len,
        ),
    )(caps, vids)


PARTS = (2, 8, 4, 8, 2)
AXES = ("z_hi", "y", "x", "z_lo", "core")
Z = ("z_hi", "z_lo")


def with_norm(tokens, norm):
    return jnp.concatenate([tokens, jnp.broadcast_to(norm[:, None, None], (1, 8, tokens.shape[2]))], axis=1)


def copies(block, count):
    return jnp.broadcast_to(block[None], (count, *block.shape))


def send(parts, axis):
    return lax.all_to_all(parts, axis, 0, 0, tiled=True)


def sum_over(parts, axis):
    return jnp.sum(send(parts, axis).astype(jnp.float32), axis=0)


def halve(kept, sent, axis, bit):
    across = [(i, i ^ (1 << bit)) for i in range(lax.axis_size(axis))]
    return kept + lax.ppermute(sent, axis, across).astype(jnp.float32)


def sum_over_bit(kept, axis, bit, dtype):
    kept = kept.reshape(-1, 2, *kept.shape[1:])
    own = (lax.axis_index(axis) >> bit) & 1
    sent = lax.dynamic_index_in_dim(kept, 1 - own, 1, keepdims=False).astype(dtype)
    return halve(lax.dynamic_index_in_dim(kept, own, 1, keepdims=False), sent, axis, bit)


def local(caption_tokens, video_tokens, row_norms, col_norms):
    q_len, v_len, features = caption_tokens.shape[1], video_tokens.shape[1], caption_tokens.shape[2]
    x_count, z_count = lax.axis_size("x"), lax.axis_size(Z)
    caps = send(copies(with_norm(caption_tokens, row_norms)[0], z_count), Z)
    vids = lax.all_gather(with_norm(video_tokens, col_norms), "core", axis=0, tiled=True)
    vids = copies(vids, lax.axis_size("y"))
    caps, vids = lax.optimization_barrier((caps, vids))
    vids = send(vids, "y").reshape(-1, *vids.shape[2:])
    caps = lax.all_gather(caps, "x", axis=0, tiled=True)
    dq, own_dq, dv_kept, dv_sent = pair_grads(caps, vids, q_len, v_len)
    dq = sum_over(dq.reshape(x_count, z_count, q_len, features), "x").astype(jnp.bfloat16)
    dv = halve(dv_kept, dv_sent, "y", 0)
    last = lax.axis_size("y").bit_length() - 2
    for bit in range(1, last):
        dv = sum_over_bit(dv, "y", bit, jnp.bfloat16)
    dq, dv = lax.optimization_barrier((dq, dv))
    dv = sum_over_bit(dv, "y", last, jnp.bfloat16)
    dv = sum_over_bit(dv, "core", 0, jnp.float32)[0].astype(jnp.bfloat16)
    dq = (sum_over(dq, Z) + own_dq).astype(jnp.bfloat16)
    return dq[None], dv[None]


def solution(mesh):
    fine = Mesh(mesh.devices.reshape(PARTS), AXES)
    return jax.shard_map(
        local,
        mesh=fine,
        in_specs=(P(AXES, None, None), P(AXES, None, None), P(AXES), P(AXES)),
        out_specs=(P(AXES, None, None), P(AXES, None, None)),
        check_vma=False,
    )
```

```python
import functools
import math

import jax
import jax.numpy as jnp
from jax import lax
from jax.experimental import pallas as pl
from jax.experimental.pallas import tpu as pltpu
from jax.sharding import Mesh
from jax.sharding import PartitionSpec as P

pool_tau = 0.05
logit_temp = 0.5


def pair_kernel(
    caps_ref, vids_ref, dq_ref, own_dq_ref, dv_kept_ref, dv_sent_ref,
    lift_ref, coef_ref, peak_ref, sum_ref, turned_ref, total_ref, mine_ref, *, q_len, v_len, lanes,
):
    cap_rows, vid_rows = caps_ref.shape[0], vids_ref.shape[0]
    features = caps_ref.shape[2]
    block_caps = lanes // q_len
    blocks = cap_rows // block_caps
    to_exp2 = 1.0 / (pool_tau * math.log(2.0))

    own_cap = lax.axis_index("x") * lax.axis_size(Z) + lax.axis_index("z_hi") * lax.axis_size("z_lo") + lax.axis_index("z_lo")
    own_vid = lax.axis_index("y") * lax.axis_size("core") + lax.axis_index("core")
    cap_bits = block_caps.bit_length() - 1
    own_block, own_place = own_cap >> cap_bits, own_cap & (block_caps - 1)

    turned_ref[...] = vids_ref[:, :v_len, :].reshape(vid_rows * v_len, features).T
    total_ref[...] = jnp.zeros_like(total_ref)

    def queries_of(block):
        return caps_ref[pl.ds(block * block_caps, block_caps), :q_len, :].reshape(lanes, features)

    def score(block):
        queries = queries_of(block)
        for v in range(vid_rows):
            scores = lax.dot_general(
                vids_ref[v, :v_len, :], queries, (((1,), (1,)), ((), ())), preferred_element_type=jnp.float32
            )
            peak = jnp.max(scores, axis=0, keepdims=True)
            lifted = jnp.exp2((scores - peak) * to_exp2)
            lift_ref[block, v] = lifted
            peak_ref[block, pl.ds(v, 1), :] = peak
            sum_ref[block, pl.ds(v, 1), :] = jnp.sum(lifted, axis=0, keepdims=True)

    q_bits = q_len.bit_length() - 1
    row = lax.broadcasted_iota(jnp.int32, (lanes, lanes), 0) >> q_bits
    col = lax.broadcasted_iota(jnp.int32, (lanes, lanes), 1) >> q_bits
    spread = jnp.where(row == col, 1.0 / (q_len * logit_temp), 0.0)
    col_norm = vids_ref[:, v_len, :1].astype(jnp.float32)
    lane_cap = lax.broadcasted_iota(jnp.int32, (vid_rows, lanes), 1) >> q_bits
    sub_vid = lax.broadcasted_iota(jnp.int32, (vid_rows, lanes), 0)

    mine_ref[...] = jnp.zeros_like(mine_ref)

    def scale(block):
        summed = sum_ref[block]
        pooled = peak_ref[block] + pool_tau * jnp.log(summed)
        logits = jnp.dot(pooled, spread, preferred_element_type=jnp.float32, precision=lax.Precision.HIGHEST)
        row_norm = jnp.zeros((1, lanes), jnp.float32)
        for c in range(block_caps):
            norm = caps_ref[block * block_caps + c, pl.ds(q_len, 1), :].astype(jnp.float32)
            norm = jnp.concatenate([norm] * (lanes // norm.shape[1]), axis=1)
            row_norm = jnp.where(lane_cap[:1] == c, norm, row_norm)
        paired = (lane_cap + block * block_caps == own_cap) & (sub_vid == own_vid)
        pair_grad = (jnp.exp(logits - row_norm) + jnp.exp(logits - col_norm) - 2.0 * paired.astype(jnp.float32)) / (2.0 * logit_temp)
        factor = pair_grad / (summed * q_len)
        sum_ref[block] = jnp.where(paired, 0.0, factor)
        mine_ref[...] += jnp.where(paired, factor, 0.0)

    def multiply(block):
        queries = queries_of(block)
        for v in range(vid_rows):
            coef_ref[pl.ds(v * v_len, v_len), :] = (lift_ref[block, v] * sum_ref[block, pl.ds(v, 1), :]).astype(jnp.bfloat16)
        coef = coef_ref[...]
        turned = jnp.dot(turned_ref[...], coef, preferred_element_type=jnp.float32)
        dq_ref[pl.ds(block * block_caps, block_caps)] = turned.T.reshape(block_caps, q_len, features).astype(dq_ref.dtype)
        total_ref[...] += jnp.dot(coef, queries, preferred_element_type=jnp.float32)

    score(0)
    scale(0)
    for block in range(1, blocks):
        score(block)
        multiply(block - 1)
        scale(block)
    multiply(blocks - 1)

    own_scale = jnp.sum(mine_ref[...], axis=0, keepdims=True)
    coef = (lift_ref[own_block, own_vid] * own_scale).astype(jnp.bfloat16)
    total_ref[pl.ds(own_vid * v_len, v_len), :] += jnp.dot(coef, queries_of(own_block), preferred_element_type=jnp.float32)
    core = lax.axis_index("core")
    for pair in range(vid_rows // 2):
        kept_at, sent_at = (2 * pair + core) * v_len, (2 * pair + 1 - core) * v_len
        dv_kept_ref[pair] = total_ref[pl.ds(pl.multiple_of(kept_at, v_len), v_len), :]
        dv_sent_ref[pair] = total_ref[pl.ds(pl.multiple_of(sent_at, v_len), v_len), :].astype(dv_sent_ref.dtype)
    total_ref[pl.ds(0, lanes), :] = lax.dot_general(
        coef, vids_ref[own_vid, :v_len, :], (((0,), (0,)), ((), ())), preferred_element_type=jnp.float32
    )
    own_dq_ref[...] = total_ref[pl.ds(own_place * q_len, q_len), :]


def pair_grads(caps, vids, q_len, v_len, lanes=256):
    cap_rows, vid_rows, features = caps.shape[0], vids.shape[0], caps.shape[2]
    blocks = cap_rows * q_len // lanes
    return pl.pallas_call(
        functools.partial(pair_kernel, q_len=q_len, v_len=v_len, lanes=lanes),
        out_shape=(
            jax.ShapeDtypeStruct((cap_rows, q_len, features), jnp.bfloat16),
            jax.ShapeDtypeStruct((q_len, features), jnp.float32),
            jax.ShapeDtypeStruct((vid_rows // 2, v_len, features), jnp.float32),
            jax.ShapeDtypeStruct((vid_rows // 2, v_len, features), jnp.bfloat16),
        ),
        in_specs=[
            pl.BlockSpec(memory_space=pltpu.VMEM),
            pl.BlockSpec(memory_space=pltpu.VMEM),
        ],
        out_specs=[pl.BlockSpec(memory_space=pltpu.VMEM)] * 4,
        scratch_shapes=[
            pltpu.VMEM((blocks, vid_rows, v_len, lanes), jnp.float32),
            pltpu.VMEM((vid_rows * v_len, lanes), jnp.bfloat16),
            pltpu.VMEM((blocks, vid_rows, lanes), jnp.float32),
            pltpu.VMEM((blocks, vid_rows, lanes), jnp.float32),
            pltpu.VMEM((features, vid_rows * v_len), jnp.bfloat16),
            pltpu.VMEM((vid_rows * v_len, features), jnp.float32),
            pltpu.VMEM((vid_rows, lanes), jnp.float32),
        ],
        compiler_params=pltpu.CompilerParams(vmem_limit_bytes=48 * 2**20),
        cost_estimate=pl.CostEstimate(
            flops=6 * cap_rows * q_len * vid_rows * v_len * features,
            bytes_accessed=4 * (cap_rows * q_len + vid_rows * v_len) * features,
            transcendentals=cap_rows * q_len * vid_rows * v_len,
        ),
    )(caps, vids)


PARTS = (2, 8, 4, 8, 2)
AXES = ("z_hi", "y", "x", "z_lo", "core")
Z = ("z_hi", "z_lo")


def with_norm(tokens, norm):
    return jnp.concatenate([tokens, jnp.broadcast_to(norm[:, None, None], (1, 8, tokens.shape[2]))], axis=1)


def copies(block, count):
    return jnp.broadcast_to(block[None], (count, *block.shape))


def send(parts, axis):
    return lax.all_to_all(parts, axis, 0, 0, tiled=True)


def sum_over(parts, axis):
    return jnp.sum(send(parts, axis).astype(jnp.float32), axis=0)


def halve(kept, sent, axis, bit):
    across = [(i, i ^ (1 << bit)) for i in range(lax.axis_size(axis))]
    return kept + lax.ppermute(sent, axis, across).astype(jnp.float32)


def sum_over_bit(kept, axis, bit):
    kept = kept.reshape(-1, 2, *kept.shape[1:])
    own = (lax.axis_index(axis) >> bit) & 1
    sent = lax.dynamic_index_in_dim(kept, 1 - own, 1, keepdims=False).astype(jnp.bfloat16)
    return halve(lax.dynamic_index_in_dim(kept, own, 1, keepdims=False), sent, axis, bit)


def local(caption_tokens, video_tokens, row_norms, col_norms):
    q_len, v_len, features = caption_tokens.shape[1], video_tokens.shape[1], caption_tokens.shape[2]
    x_count, z_count = lax.axis_size("x"), lax.axis_size(Z)
    caps = send(copies(with_norm(caption_tokens, row_norms)[0], z_count), Z)
    vids = lax.all_gather(with_norm(video_tokens, col_norms), "core", axis=0, tiled=True)
    vids = copies(vids, lax.axis_size("y"))
    caps, vids = lax.optimization_barrier((caps, vids))
    vids = send(vids, "y").reshape(-1, *vids.shape[2:])
    caps = lax.all_gather(caps, "x", axis=0, tiled=True)
    dq, own_dq, dv_kept, dv_sent = pair_grads(caps, vids, q_len, v_len)
    dq = sum_over(dq.reshape(x_count, z_count, q_len, features), "x").astype(jnp.bfloat16)
    dv = halve(dv_kept, dv_sent, "core", 0)
    last = lax.axis_size("y").bit_length() - 2
    for bit in range(last):
        dv = sum_over_bit(dv, "y", bit)
    dq, dv = lax.optimization_barrier((dq, dv))
    dv = sum_over_bit(dv, "y", last)[0].astype(jnp.bfloat16)
    dq = (sum_over(dq, Z) + own_dq).astype(jnp.bfloat16)
    return dq[None], dv[None]


def solution(mesh):
    fine = Mesh(mesh.devices.reshape(PARTS), AXES)
    return jax.shard_map(
        local,
        mesh=fine,
        in_specs=(P(AXES, None, None), P(AXES, None, None), P(AXES), P(AXES)),
        out_specs=(P(AXES, None, None), P(AXES, None, None)),
        check_vma=False,
    )
```

```python
import functools
import math

import jax
import jax.numpy as jnp
from jax import lax
from jax.experimental import pallas as pl
from jax.experimental.pallas import tpu as pltpu
from jax.sharding import Mesh
from jax.sharding import PartitionSpec as P

pool_tau = 0.05
logit_temp = 0.5


def pair_kernel(
    caps_ref, vids_ref, dq_ref, own_dq_ref, dv_kept_ref, dv_sent_ref,
    lift_ref, coef_ref, peak_ref, sum_ref, turned_ref, total_ref, mine_ref, *, q_len, v_len, lanes,
):
    cap_rows, vid_rows = caps_ref.shape[0], vids_ref.shape[0]
    features = caps_ref.shape[2]
    block_caps = lanes // q_len
    blocks = cap_rows // block_caps
    to_exp2 = 1.0 / (pool_tau * math.log(2.0))

    own_cap = lax.axis_index("x") * lax.axis_size(Z) + lax.axis_index("z_hi") * lax.axis_size("z_lo") + lax.axis_index("z_lo")
    own_vid = lax.axis_index("y") * lax.axis_size("core") + lax.axis_index("core")
    cap_bits = block_caps.bit_length() - 1
    own_block, own_place = own_cap >> cap_bits, own_cap & (block_caps - 1)

    turned_ref[...] = vids_ref[:, :v_len, :].reshape(vid_rows * v_len, features).T
    total_ref[...] = jnp.zeros_like(total_ref)

    def queries_of(block):
        return caps_ref[pl.ds(block * block_caps, block_caps), :q_len, :].reshape(lanes, features)

    def score(block):
        queries = queries_of(block)
        for v in range(vid_rows):
            scores = lax.dot_general(
                vids_ref[v, :v_len, :], queries, (((1,), (1,)), ((), ())), preferred_element_type=jnp.float32
            )
            peak = jnp.max(scores, axis=0, keepdims=True)
            lifted = jnp.exp2((scores - peak) * to_exp2)
            lift_ref[block, v] = lifted
            peak_ref[block, pl.ds(v, 1), :] = peak
            sum_ref[block, pl.ds(v, 1), :] = jnp.sum(lifted, axis=0, keepdims=True)

    q_bits = q_len.bit_length() - 1
    row = lax.broadcasted_iota(jnp.int32, (lanes, lanes), 0) >> q_bits
    col = lax.broadcasted_iota(jnp.int32, (lanes, lanes), 1) >> q_bits
    spread = jnp.where(row == col, 1.0 / (q_len * logit_temp), 0.0)
    col_norm = vids_ref[:, v_len, :1].astype(jnp.float32)
    lane_cap = lax.broadcasted_iota(jnp.int32, (vid_rows, lanes), 1) >> q_bits
    sub_vid = lax.broadcasted_iota(jnp.int32, (vid_rows, lanes), 0)

    mine_ref[...] = jnp.zeros_like(mine_ref)

    def scale(block):
        summed = sum_ref[block]
        pooled = peak_ref[block] + pool_tau * jnp.log(summed)
        logits = jnp.dot(pooled, spread, preferred_element_type=jnp.float32, precision=lax.Precision.HIGHEST)
        row_norm = jnp.zeros((1, lanes), jnp.float32)
        for c in range(block_caps):
            norm = caps_ref[block * block_caps + c, pl.ds(q_len, 1), :].astype(jnp.float32)
            norm = jnp.concatenate([norm] * (lanes // norm.shape[1]), axis=1)
            row_norm = jnp.where(lane_cap[:1] == c, norm, row_norm)
        paired = (lane_cap + block * block_caps == own_cap) & (sub_vid == own_vid)
        pair_grad = (jnp.exp(logits - row_norm) + jnp.exp(logits - col_norm) - 2.0 * paired.astype(jnp.float32)) / (2.0 * logit_temp)
        factor = pair_grad / (summed * q_len)
        sum_ref[block] = jnp.where(paired, 0.0, factor)
        mine_ref[...] += jnp.where(paired, factor, 0.0)

    def multiply(block):
        queries = queries_of(block)
        for v in range(vid_rows):
            coef_ref[pl.ds(v * v_len, v_len), :] = (lift_ref[block, v] * sum_ref[block, pl.ds(v, 1), :]).astype(jnp.bfloat16)
        coef = coef_ref[...]
        turned = jnp.dot(turned_ref[...], coef, preferred_element_type=jnp.float32)
        dq_ref[pl.ds(block * block_caps, block_caps)] = turned.T.reshape(block_caps, q_len, features).astype(dq_ref.dtype)
        total_ref[...] += jnp.dot(coef, queries, preferred_element_type=jnp.float32)

    score(0)
    scale(0)
    for block in range(1, blocks):
        score(block)
        multiply(block - 1)
        scale(block)
    multiply(blocks - 1)

    own_scale = jnp.sum(mine_ref[...], axis=0, keepdims=True)
    coef = (lift_ref[own_block, own_vid] * own_scale).astype(jnp.bfloat16)
    total_ref[pl.ds(own_vid * v_len, v_len), :] += jnp.dot(coef, queries_of(own_block), preferred_element_type=jnp.float32)
    bit = lax.axis_index("y") & 1
    for pair in range(vid_rows // 2):
        high, core = divmod(pair, 2)
        kept_at, sent_at = (4 * high + 2 * bit + core) * v_len, (4 * high + 2 - 2 * bit + core) * v_len
        dv_kept_ref[pair] = total_ref[pl.ds(pl.multiple_of(kept_at, v_len), v_len), :]
        dv_sent_ref[pair] = total_ref[pl.ds(pl.multiple_of(sent_at, v_len), v_len), :].astype(dv_sent_ref.dtype)
    total_ref[pl.ds(0, lanes), :] = lax.dot_general(
        coef, vids_ref[own_vid, :v_len, :], (((0,), (0,)), ((), ())), preferred_element_type=jnp.float32
    )
    own_dq_ref[...] = total_ref[pl.ds(own_place * q_len, q_len), :]


def pair_grads(caps, vids, q_len, v_len, lanes=256):
    cap_rows, vid_rows, features = caps.shape[0], vids.shape[0], caps.shape[2]
    blocks = cap_rows * q_len // lanes
    return pl.pallas_call(
        functools.partial(pair_kernel, q_len=q_len, v_len=v_len, lanes=lanes),
        out_shape=(
            jax.ShapeDtypeStruct((cap_rows, q_len, features), jnp.bfloat16),
            jax.ShapeDtypeStruct((q_len, features), jnp.float32),
            jax.ShapeDtypeStruct((vid_rows // 2, v_len, features), jnp.float32),
            jax.ShapeDtypeStruct((vid_rows // 2, v_len, features), jnp.bfloat16),
        ),
        in_specs=[
            pl.BlockSpec(memory_space=pltpu.VMEM),
            pl.BlockSpec(memory_space=pltpu.VMEM),
        ],
        out_specs=[pl.BlockSpec(memory_space=pltpu.VMEM)] * 4,
        scratch_shapes=[
            pltpu.VMEM((blocks, vid_rows, v_len, lanes), jnp.float32),
            pltpu.VMEM((vid_rows * v_len, lanes), jnp.bfloat16),
            pltpu.VMEM((blocks, vid_rows, lanes), jnp.float32),
            pltpu.VMEM((blocks, vid_rows, lanes), jnp.float32),
            pltpu.VMEM((features, vid_rows * v_len), jnp.bfloat16),
            pltpu.VMEM((vid_rows * v_len, features), jnp.float32),
            pltpu.VMEM((vid_rows, lanes), jnp.float32),
        ],
        compiler_params=pltpu.CompilerParams(vmem_limit_bytes=48 * 2**20),
        cost_estimate=pl.CostEstimate(
            flops=6 * cap_rows * q_len * vid_rows * v_len * features,
            bytes_accessed=4 * (cap_rows * q_len + vid_rows * v_len) * features,
            transcendentals=cap_rows * q_len * vid_rows * v_len,
        ),
    )(caps, vids)


PARTS = (2, 8, 4, 8, 2)
AXES = ("z_hi", "y", "x", "z_lo", "core")
Z = ("z_hi", "z_lo")


def with_norm(tokens, norm):
    return jnp.concatenate([tokens, jnp.broadcast_to(norm[:, None, None], (1, 8, tokens.shape[2]))], axis=1)


def copies(block, count):
    return jnp.broadcast_to(block[None], (count, *block.shape))


def send(parts, axis):
    return lax.all_to_all(parts, axis, 0, 0, tiled=True)


def sum_over(parts, axis):
    return jnp.sum(send(parts, axis).astype(jnp.float32), axis=0)


def halve(kept, sent, axis, bit):
    across = [(i, i ^ (1 << bit)) for i in range(lax.axis_size(axis))]
    return kept + lax.ppermute(sent, axis, across).astype(jnp.float32)


def sum_over_bit(kept, axis, bit):
    kept = kept.reshape(-1, 2, *kept.shape[1:])
    own = (lax.axis_index(axis) >> bit) & 1
    sent = lax.dynamic_index_in_dim(kept, 1 - own, 1, keepdims=False).astype(jnp.bfloat16)
    return halve(lax.dynamic_index_in_dim(kept, own, 1, keepdims=False), sent, axis, bit)


def local(caption_tokens, video_tokens, row_norms, col_norms):
    q_len, v_len, features = caption_tokens.shape[1], video_tokens.shape[1], caption_tokens.shape[2]
    x_count, z_count = lax.axis_size("x"), lax.axis_size(Z)
    caps = send(copies(with_norm(caption_tokens, row_norms)[0], z_count), Z)
    vids = lax.all_gather(with_norm(video_tokens, col_norms), "core", axis=0, tiled=True)
    vids = copies(vids, lax.axis_size("y"))
    caps, vids = lax.optimization_barrier((caps, vids))
    vids = send(vids, "y").reshape(-1, *vids.shape[2:])
    caps = lax.all_gather(caps, "x", axis=0, tiled=True)
    dq, own_dq, dv_kept, dv_sent = pair_grads(caps, vids, q_len, v_len)
    dq = sum_over(dq.reshape(x_count, z_count, q_len, features), "x").astype(jnp.bfloat16)
    dv = halve(dv_kept, dv_sent, "y", 0)
    dv = sum_over_bit(dv, "core", 0)
    last = lax.axis_size("y").bit_length() - 2
    for bit in range(1, last):
        dv = sum_over_bit(dv, "y", bit)
    dq, dv = lax.optimization_barrier((dq, dv))
    dv = sum_over_bit(dv, "y", last)[0].astype(jnp.bfloat16)
    dq = (sum_over(dq, Z) + own_dq).astype(jnp.bfloat16)
    return dq[None], dv[None]


def solution(mesh):
    fine = Mesh(mesh.devices.reshape(PARTS), AXES)
    return jax.shard_map(
        local,
        mesh=fine,
        in_specs=(P(AXES, None, None), P(AXES, None, None), P(AXES), P(AXES)),
        out_specs=(P(AXES, None, None), P(AXES, None, None)),
        check_vma=False,
    )
```
